32 devices in a mesh: groups: 2 (over x), latent: 16 (over z, y, core).
Axes of the slice: x: 2, y: 2, z: 4, core: 2. Of those that a mesh axis runs over, the one named last changes fastest.
Arguments:
- row_store: bfloat16 [1024, 2, 4608], P(('groups', 'latent')), parts along dimension 0, may hold values from -6 to 6
- row_slot: int32 [512], P('groups'), parts along dimension 0, may hold values from 0 to 511, as said below
- targets: bfloat16 [512, 2, 4608], P(('groups', 'latent')), parts along dimension 0, may hold values from -6 to 6
- enc_weight: bfloat16 [4, 4608, 2048], P('groups', None, 'latent'), parts along dimension 0, may hold values from -0.09375 to 0.09375
- enc_bias: float32 [4, 2048], P('groups', 'latent'), parts along dimension 0, may hold values from -1 to 1
- dec_weight: bfloat16 [6, 2048, 4608], P('groups', 'latent'), parts along dimension 0, may hold values from -0.125 to 0.125
- dec_bias: float32 [4, 4608], P('groups'), parts along dimension 0, may hold values from -5 to 5
Outputs:
- rebuilt: float32 [512, 2, 4608], P(('groups', 'latent')), parts along dimension 0
- grad_enc: bfloat16 [4, 4608, 2048], P('groups', None, 'latent'), parts along dimension 0
- grad_ebias: float32 [4, 2048], P('groups', 'latent'), parts along dimension 0
- grad_dec: bfloat16 [6, 2048, 4608], P('groups', 'latent'), parts along dimension 0
- grad_dbias: float32 [4, 4608], P('groups'), parts along dimension 0
The draws below stay inside these ranges and needn't reach their ends.
There are 2 independent parts, one for each index of `groups`. The reference program is written for one: setup_inputs(seed, part) draws one part's arguments, and reference() takes and returns one part's arrays. A program takes and returns all parts, laid end to end along the dimension named above; each array names one. Nothing has to cross between parts.
Inputs may be any that keep to these rules, and one draw needn't show every extreme that they name: The slots row_slot holds are distinct. Slot k belongs to owner k // 32; an owner's slots of this batch are its first ones in a row, with no gap. Owners hold 0 to 32 rows of the batch, and in every draw some owner holds exactly 32.
All inputs are finite; a program needn't handle non-finite values.
Results may differ from the reference program's by a relative error of at most 0.0058.
Values may be sent and summed in bfloat16 or wider, within the bound.
A program may use at most 128 MiB of HBM per device.

```python
import math
import jax
import jax.numpy as jnp
from jax import lax

D = 4608
LAYERS = 2
ROWS = 256
LATENTS = 2048
PAIRS = 3
ROWS_DEV = 16
STORE_CAP = 32
N_LATENT = 16


def draw_row_slot(key, part):
    key = jax.random.fold_in(key, 11)
    first_key, second_key, third_key = jax.random.split(key, 3)
    half_count = N_LATENT // 2
    shifts = jax.random.randint(first_key, (half_count,), -(ROWS_DEV - 1), ROWS_DEV)
    shifts = shifts.at[0].set(ROWS_DEV)
    shifts = shifts.at[half_count - 1].set(ROWS_DEV)
    paired = jnp.stack([ROWS_DEV + shifts, ROWS_DEV - shifts], axis=1).reshape(-1)
    others = jax.random.permutation(second_key, N_LATENT - 1) + 1
    ordering = jnp.concatenate([others, jnp.zeros((1,), jnp.int32)])
    counts = paired[ordering]
    first_full = jnp.argmax((counts > 0).astype(jnp.int32)).astype(jnp.int32)
    head_count = counts[0]
    found_count = counts[first_full]
    counts = counts.at[0].set(found_count)
    counts = counts.at[first_full].set(head_count)
    ends = jnp.cumsum(counts)
    starts = ends - counts
    position = jnp.arange(ROWS, dtype=jnp.int32)
    owners = jnp.sum((ends[None, :] <= position[:, None]).astype(jnp.int32), axis=1)
    slots = owners * STORE_CAP + position - starts[owners]
    shuffle = jax.random.permutation(third_key, ROWS)
    return slots[shuffle].astype(jnp.int32)


def shard_levels(key, shape, cuts, least, top_value):
    factor_of = 1.0
    for dim, shards_of in cuts:
        steps = jax.random.uniform(jax.random.fold_in(jax.random.fold_in(key, 6), dim), (shards_of,), jnp.float32, least / len(cuts), top_value / len(cuts))
        factor_of = factor_of * jnp.repeat(jnp.exp(steps), shape[dim] // shards_of).reshape((-1,) + (1,) * (len(shape) - 1 - dim))
    return factor_of


def noise(own_key, extent, width, limit, cuts=(), kind=jnp.bfloat16):
    entries = jax.random.normal(own_key, extent, jnp.float32) * width
    if len(cuts) > 0:
        entries = shard_levels(own_key, extent, cuts, -0.22, 0.18) * entries
    return jnp.clip(entries, min=-limit, max=limit).astype(kind)


def setup_inputs(seed: int = 0, part: int = 0) -> dict:
    seeds = jax.random.split(jax.random.key(seed), 8)
    part_splits = jax.random.split(jax.random.fold_in(seeds[7], part), 8)
    row_store = noise(part_splits[0], (N_LATENT * STORE_CAP, LAYERS, D), 1.0, 6.0, ((0, 16),))
    row_slot = draw_row_slot(jax.random.fold_in(jax.random.fold_in(seeds[7], part), 71), part)
    targets = noise(part_splits[2], (ROWS, LAYERS, D), 1.0, 6.0, ((0, 16),))
    enc_weight = noise(part_splits[3], (LAYERS, D, LATENTS), D ** -0.5, 0.09375, ((2, 16),))
    enc_bias = jnp.clip(jax.random.uniform(part_splits[4], (LAYERS, LATENTS), jnp.float32, -1.0, 1.0) * shard_levels(part_splits[4], (LAYERS, LATENTS), ((1, 16),), -0.4, 0.0), -1.0, 1.0)
    dec_weight = noise(part_splits[5], (PAIRS, LATENTS, D), LATENTS ** -0.5, 0.125, ((1, 16),))
    dec_bias = noise(part_splits[6], (LAYERS, D), 1.0, 5.0, (), jnp.float32)
    return {"row_store": row_store, "row_slot": row_slot, "targets": targets, "enc_weight": enc_weight, "enc_bias": enc_bias, "dec_weight": dec_weight, "dec_bias": dec_bias}


def pair_index(source, target, layers):
    return source * layers - source * (source - 1) // 2 + target - source

def activate(values):
    return jax.nn.gelu(values, approximate=True)

def reference(row_store, row_slot, targets, enc_weight, enc_bias, dec_weight, dec_bias):
    inputs = jnp.take(row_store, row_slot, axis=0)
    pre_list = []
    latents = []
    for source in range(LAYERS):
        pre_acts = jnp.dot(inputs[:, source], enc_weight[source], preferred_element_type=jnp.float32) + enc_bias[source][None, :]
        pre_list.append(pre_acts)
        latents.append(activate(pre_acts).astype(jnp.bfloat16))
    rebuilt_list = []
    for target in range(LAYERS):
        summed_terms = jnp.zeros((ROWS, D), jnp.float32)
        for source in range(target + 1):
            summed_terms = summed_terms + jnp.dot(latents[source], dec_weight[pair_index(source, target, LAYERS)], preferred_element_type=jnp.float32)
        rebuilt_list.append(summed_terms + dec_bias[target][None, :])
    rebuilt = jnp.stack(rebuilt_list, axis=1)
    factor = 1.0 / math.sqrt(ROWS)
    errors = ((rebuilt - targets.astype(jnp.float32)) * factor).astype(jnp.bfloat16)
    grad_dec_list = []
    for source in range(LAYERS):
        for target in range(source, LAYERS):
            grad_dec_list.append(jnp.dot(latents[source].T, errors[:, target], preferred_element_type=jnp.float32).astype(jnp.bfloat16))
    grad_dec = jnp.stack(grad_dec_list, axis=0)
    grad_dbias = lax.optimization_barrier(jnp.sum(errors.astype(jnp.float32), axis=0))
    grad_enc_list = []
    grad_ebias_list = []
    for source in range(LAYERS):
        back = jnp.zeros((ROWS, LATENTS), jnp.float32)
        for target in range(source, LAYERS):
            back = back + jnp.dot(errors[:, target], dec_weight[pair_index(source, target, LAYERS)].T, preferred_element_type=jnp.float32)
        unused, pullback = jax.vjp(activate, pre_list[source])
        dpre = pullback(back)[0]
        grad_ebias_list.append(lax.optimization_barrier(jnp.sum(dpre, axis=0)))
        grad_enc_list.append(jnp.dot(inputs[:, source].T, dpre.astype(jnp.bfloat16), preferred_element_type=jnp.float32).astype(jnp.bfloat16))
    grad_enc = jnp.stack(grad_enc_list, axis=0)
    grad_ebias = jnp.stack(grad_ebias_list, axis=0)
    return (rebuilt, grad_enc, grad_ebias, grad_dec, grad_dbias)
```

```python
import functools
import math

import jax
import jax.numpy as jnp
from jax import lax
from jax.experimental import pallas as pl
from jax.experimental.pallas import tpu as pltpu
from jax.sharding import PartitionSpec as P

MESH = pl.DeviceIdType.MESH
VMEM_LIMIT = 56 * 1024 * 1024


def pair_index(source, target, layers):
    return source * layers - source * (source - 1) // 2 + target - source


def activate(values):
    return jax.nn.gelu(values, approximate=True)


def recon_terms(target, latents, dec_weight, layers):
    summed_terms = None
    for source in range(target + 1):
        product = jnp.dot(
            latents[source],
            dec_weight[pair_index(source, target, layers)],
            preferred_element_type=jnp.float32,
        )
        summed_terms = product if summed_terms is None else summed_terms + product
    return summed_terms


def position():
    me = lax.axis_index("latent")
    return me // 4, (me // 2) % 2, me % 2


def greet(long, z, y, c):
    barrier = pltpu.get_barrier_semaphore()

    def signal(zz, yy, cc):
        pl.semaphore_signal(
            barrier, inc=1, device_id={"latent": zz * 4 + yy * 2 + cc}, device_id_type=MESH
        )

    signal(z, y, 1 - c)
    signal(z, 1 - y, c)

    @pl.when(z > 0)
    def _():
        signal(z - 1, y, c)

    @pl.when(z < long - 1)
    def _():
        signal(z + 1, y, c)

    peers = 2 + (z > 0).astype(jnp.int32) + (z < long - 1).astype(jnp.int32)
    pl.semaphore_wait(barrier, peers)


def gather_steps(long, rows, z, y, c, whole, first_ref, send_sem, recv_sem):
    def index(zz, yy, cc):
        return zz * 4 + yy * 2 + cc

    def block(owner):
        return whole.at[:, pl.ds(pl.multiple_of(owner * rows, rows), rows), :]

    def copy(kind, owner, target, src=None):
        return pltpu.make_async_remote_copy(
            src_ref=block(owner) if src is None else src,
            dst_ref=block(owner),
            send_sem=send_sem.at[kind, owner],
            recv_sem=recv_sem.at[owner],
            device_id={"latent": target},
            device_id_type=MESH,
        )

    me = index(z, y, c)
    left, right = index(z - 1, y, c), index(z + 1, y, c)
    across, twin = index(z, 1 - y, c), index(z, y, 1 - c)

    def arrived(owner):
        copy(0, owner, twin).wait_recv()

    def guarded(condition, act):
        pl.when(condition)(act)

    guarded(z < long - 1, lambda: copy(0, me, right, first_ref).start())
    guarded(z > 0, lambda: copy(1, me, left, first_ref).start())
    copy(2, me, across, first_ref).start()
    copy(3, me, twin, first_ref).start()

    def line_arrival(step):
        def from_left():
            owner = index(z - step, y, c)
            arrived(owner)
            guarded(z < long - 1, lambda: copy(0, owner, right).start())
            copy(2, owner, across).start()
            copy(3, owner, twin).start()

        def from_right():
            owner = index(z + step, y, c)
            arrived(owner)
            guarded(z > 0, lambda: copy(1, owner, left).start())
            copy(2, owner, across).start()
            copy(3, owner, twin).start()

        guarded(z - step >= 0, from_left)
        guarded(z + step <= long - 1, from_right)

    def across_arrival(step):
        def take(zz):
            owner = index(zz, 1 - y, c)
            arrived(owner)
            copy(3, owner, twin).start()

        if step == 0:
            take(z)
        else:
            guarded(z - step >= 0, lambda: take(z - step))
            guarded(z + step <= long - 1, lambda: take(z + step))

    for step in range(1, long):
        line_arrival(step)
        across_arrival(step - 1)
    across_arrival(long - 1)
    for zz in range(long):
        for yy in range(2):
            arrived(index(zz, yy, 1 - c))

    for zz in range(long):
        own = index(zz, y, c)
        guarded(jnp.logical_and(z < long - 1, zz <= z), lambda own=own: copy(0, own, right).wait_send())
        guarded(jnp.logical_and(z > 0, zz >= z), lambda own=own: copy(1, own, left).wait_send())
        copy(2, own, across).wait_send()
        copy(3, own, twin).wait_send()
        copy(3, index(zz, 1 - y, c), twin).wait_send()


def gather_kernel(n, own_ref, whole_ref, send_sem, recv_sem, local_sem):
    long = n // 4
    rows = own_ref.shape[1]
    z, y, c = position()
    greet(long, z, y, c)
    me = z * 4 + y * 2 + c
    local = pltpu.make_async_copy(
        own_ref,
        whole_ref.at[:, pl.ds(pl.multiple_of(me * rows, rows), rows), :],
        local_sem,
    )
    local.start()
    gather_steps(long, rows, z, y, c, whole_ref, own_ref, send_sem, recv_sem)
    local.wait()


def gather_rows(own, n, collective_id):
    layers, rows, width = own.shape
    return pl.pallas_call(
        functools.partial(gather_kernel, n),
        out_shape=jax.ShapeDtypeStruct((layers, n * rows, width), own.dtype),
        in_specs=[pl.BlockSpec(memory_space=pl.ANY)],
        out_specs=pl.BlockSpec(memory_space=pl.ANY),
        scratch_shapes=[
            pltpu.SemaphoreType.DMA((4, n)),
            pltpu.SemaphoreType.DMA((n,)),
            pltpu.SemaphoreType.DMA,
        ],
        compiler_params=pltpu.CompilerParams(
            collective_id=collective_id, has_side_effects=True, vmem_limit_bytes=VMEM_LIMIT
        ),
        name=f"gather_rows_{rows}",
    )(own)


def scatter_kernel(
    n, part_ref, sum_ref, core_buf, y_out, y_in, right_out, right_in, left_out, left_in,
    core_send, core_recv, y_send, y_recv, right_send, right_recv, left_send, left_recv,
):
    long = n // 4
    layers, rows, width = sum_ref.shape
    z, y, c = position()
    greet(long, z, y, c)
    f32 = jnp.float32

    def index(zz, yy, cc):
        return zz * 4 + yy * 2 + cc

    def rows_of(owner):
        return pl.ds(pl.multiple_of(owner * rows, rows), rows)

    def remote(src, dst, send, recv, target):
        return pltpu.make_async_remote_copy(
            src_ref=src, dst_ref=dst, send_sem=send, recv_sem=recv,
            device_id={"latent": target}, device_id_type=MESH,
        )

    order = []
    low, high = 0, long - 1
    while low <= high:
        order.append(high)
        if low < high:
            order.append(low)
        low, high = low + 1, high - 1
    pieces = [(zz, t) for zz in order for t in range(layers)]

    def core_copy(zz, side, t):
        owner = index(zz, 1 - y if side == 0 else y, 1 - c)
        return remote(
            part_ref.at[t, rows_of(owner), :], core_buf.at[side, zz, t],
            core_send.at[side, zz, t], core_recv.at[side, zz, t], index(z, y, 1 - c),
        )

    def y_copy(zz, t):
        return remote(
            y_out.at[zz, t], y_in.at[zz, t], y_send.at[zz, t], y_recv.at[zz, t],
            index(z, 1 - y, c),
        )

    def right_copy(zz, t):
        return remote(
            right_out.at[zz, t], right_in.at[zz, t], right_send.at[zz, t], right_recv.at[zz, t],
            index(z + 1, y, c),
        )

    def left_copy(zz, t):
        return remote(
            left_out.at[zz, t], left_in.at[zz, t], left_send.at[zz, t], left_recv.at[zz, t],
            index(z - 1, y, c),
        )

    for side in range(2):
        for zz, t in pieces:
            core_copy(zz, side, t).start()

    def start_y(piece):
        zz, t = piece
        core_copy(zz, 0, t).wait_recv()
        owner = index(zz, 1 - y, c)
        total = part_ref[t, rows_of(owner), :].astype(f32) + core_buf[0, zz, t].astype(f32)
        y_out[zz, t] = total.astype(y_out.dtype)
        y_copy(zz, t).start()

    ahead = 2
    for piece in pieces[:ahead]:
        start_y(piece)
    for number, (zz, t) in enumerate(pieces):
        core_copy(zz, 1, t).wait_recv()
        y_copy(zz, t).wait_recv()
        if number + ahead < len(pieces):
            start_y(pieces[number + ahead])

        def here(zz=zz, t=t):
            owner = index(zz, y, c)
            return (
                part_ref[t, rows_of(owner), :].astype(f32)
                + core_buf[1, zz, t].astype(f32)
                + y_in[zz, t].astype(f32)
            )

        @pl.when(zz == z)
        def _():
            sum_ref[t] = here()

        @pl.when(zz > z)
        def _():
            @pl.when(z == 0)
            def _():
                right_out[zz, t] = here().astype(right_out.dtype)

            @pl.when(z > 0)
            def _():
                right_copy(zz, t).wait_recv()
                right_out[zz, t] = (here() + right_in[zz, t].astype(f32)).astype(right_out.dtype)

            right_copy(zz, t).start()

        @pl.when(zz < z)
        def _():
            @pl.when(z == long - 1)
            def _():
                left_out[zz, t] = here().astype(left_out.dtype)

            @pl.when(z < long - 1)
            def _():
                left_copy(zz, t).wait_recv()
                left_out[zz, t] = (here() + left_in[zz, t].astype(f32)).astype(left_out.dtype)

            left_copy(zz, t).start()

    for t in range(layers):
        @pl.when(z > 0)
        def _():
            right_copy(z, t).wait_recv()
            sum_ref[t] += right_in[z, t].astype(f32)

        @pl.when(z < long - 1)
        def _():
            left_copy(z, t).wait_recv()
            sum_ref[t] += left_in[z, t].astype(f32)

    for zz, t in pieces:
        core_copy(zz, 0, t).wait_send()
        core_copy(zz, 1, t).wait_send()
        y_copy(zz, t).wait_send()
        pl.when(zz > z)(lambda zz=zz, t=t: right_copy(zz, t).wait_send())
        pl.when(zz < z)(lambda zz=zz, t=t: left_copy(zz, t).wait_send())


def scatter_sum(parts, n, collective_id):
    layers, all_rows, width = parts.shape
    rows, long = all_rows // n, n // 4
    line = pltpu.VMEM((long, layers, rows, width), parts.dtype)
    sems = pltpu.SemaphoreType.DMA((long, layers))
    two_sems = pltpu.SemaphoreType.DMA((2, long, layers))
    return pl.pallas_call(
        functools.partial(scatter_kernel, n),
        out_shape=jax.ShapeDtypeStruct((layers, rows, width), jnp.float32),
        in_specs=[pl.BlockSpec(memory_space=pltpu.VMEM)],
        out_specs=pl.BlockSpec(memory_space=pltpu.VMEM),
        scratch_shapes=[
            pltpu.VMEM((2, long, layers, rows, width), parts.dtype),
            line, line, line, line, line, line,
            two_sems, two_sems, sems, sems, sems, sems, sems, sems,
        ],
        compiler_params=pltpu.CompilerParams(
            collective_id=collective_id, has_side_effects=True, vmem_limit_bytes=VMEM_LIMIT
        ),
        name="scatter_sum",
    )(parts)


def plain_gather(own):
    return lax.all_gather(own, "latent", axis=1, tiled=True)


def body(n, row_store, row_slot, targets, enc_weight, enc_bias, dec_weight, dec_bias):
    layers = enc_weight.shape[0]
    row_count = row_slot.shape[0]
    own_rows = targets.shape[0]
    f32, bf16 = jnp.float32, jnp.bfloat16
    by_kernel = n % 4 == 0 and row_store.shape[0] % 16 == 0 and own_rows % 16 == 0

    store = jnp.transpose(row_store, (1, 0, 2))
    slots = gather_rows(store, n, 0) if by_kernel else plain_gather(store)
    slot_count = slots.shape[1]
    pick = row_slot[:, None] == jnp.arange(slot_count, dtype=row_slot.dtype)[None, :]
    slot_pre = jnp.concatenate(
        [
            jnp.dot(slots[source], enc_weight[source], preferred_element_type=f32)
            for source in range(layers)
        ],
        axis=1,
    )
    row_pre = jnp.dot(
        pick.astype(f32), slot_pre, precision=lax.Precision.HIGHEST, preferred_element_type=f32
    )
    wide = enc_weight.shape[2]
    pre_list = []
    latents = []
    for source in range(layers):
        pre_acts = row_pre[:, source * wide : (source + 1) * wide] + enc_bias[source][None, :]
        pre_list.append(pre_acts)
        latents.append(activate(pre_acts).astype(bf16))
    terms = [recon_terms(target, latents, dec_weight, layers) for target in range(layers)]
    if by_kernel:
        summed = scatter_sum(jnp.stack([term.astype(bf16) for term in terms], axis=0), n, 1)
    else:
        summed = lax.psum_scatter(
            jnp.stack(terms, axis=0), "latent", scatter_dimension=1, tiled=True
        )
    rebuilt = summed + dec_bias[:, None, :]
    factor = 1.0 / math.sqrt(row_count)
    wanted = jnp.transpose(targets, (1, 0, 2)).astype(f32)
    error_part = ((rebuilt - wanted) * factor).astype(bf16)
    errors = gather_rows(error_part, n, 2) if by_kernel else plain_gather(error_part)
    grad_dec_list = []
    for source in range(layers):
        for target in range(source, layers):
            grad_dec_list.append(
                jnp.dot(latents[source].T, errors[target], preferred_element_type=f32).astype(bf16)
            )
    grad_dec = jnp.stack(grad_dec_list, axis=0)
    grad_dbias = jnp.sum(errors.astype(f32), axis=1)
    grad_ebias_list = []
    low_list = []
    for source in range(layers):
        back = None
        for target in range(source, layers):
            product = lax.dot_general(
                errors[target],
                dec_weight[pair_index(source, target, layers)],
                (((1,), (1,)), ((), ())),
                preferred_element_type=f32,
            )
            back = product if back is None else back + product
        unused, pullback = jax.vjp(activate, pre_list[source])
        dpre = pullback(back)[0]
        grad_ebias_list.append(jnp.sum(dpre, axis=0))
        low_list.append(dpre.astype(bf16))
    slot_dpre = lax.dot_general(
        pick.astype(bf16),
        jnp.concatenate(low_list, axis=1),
        (((0,), (0,)), ((), ())),
        preferred_element_type=f32,
    ).astype(bf16)
    grad_enc = jnp.stack(
        [
            lax.dot_general(
                slots[source],
                slot_dpre[:, source * wide : (source + 1) * wide],
                (((0,), (0,)), ((), ())),
                preferred_element_type=f32,
            ).astype(bf16)
            for source in range(layers)
        ],
        axis=0,
    )
    grad_ebias = jnp.stack(grad_ebias_list, axis=0)
    return (jnp.transpose(rebuilt, (1, 0, 2)), grad_enc, grad_ebias, grad_dec, grad_dbias)


def solution(mesh):
    in_specs = (
        P(("groups", "latent"), None, None),
        P("groups"),
        P(("groups", "latent"), None, None),
        P("groups", None, "latent"),
        P("groups", "latent"),
        P("groups", "latent", None),
        P("groups", None),
    )
    out_specs = (
        P(("groups", "latent"), None, None),
        P("groups", None, "latent"),
        P("groups", "latent"),
        P("groups", "latent", None),
        P("groups", None),
    )
    return jax.shard_map(
        functools.partial(body, mesh.shape["latent"]),
        mesh=mesh,
        in_specs=in_specs,
        out_specs=out_specs,
        check_vma=False,
    )
```

```python
import functools
import math

import jax
import jax.numpy as jnp
from jax import lax
from jax.experimental import pallas as pl
from jax.experimental.pallas import tpu as pltpu
from jax.sharding import PartitionSpec as P

MESH = pl.DeviceIdType.MESH
VMEM_LIMIT = 56 * 1024 * 1024


def pair_index(source, target, layers):
    return source * layers - source * (source - 1) // 2 + target - source


def activate(values):
    return jax.nn.gelu(values, approximate=True)


def recon_terms(target, latents, dec_weight, layers):
    summed_terms = None
    for source in range(target + 1):
        product = jnp.dot(
            latents[source],
            dec_weight[pair_index(source, target, layers)],
            preferred_element_type=jnp.float32,
        )
        summed_terms = product if summed_terms is None else summed_terms + product
    return summed_terms


def position():
    me = lax.axis_index("latent")
    return me // 4, (me // 2) % 2, me % 2


def greet(long, z, y, c):
    barrier = pltpu.get_barrier_semaphore()

    def signal(zz, yy, cc):
        pl.semaphore_signal(
            barrier, inc=1, device_id={"latent": zz * 4 + yy * 2 + cc}, device_id_type=MESH
        )

    signal(z, y, 1 - c)
    signal(z, 1 - y, c)

    @pl.when(z > 0)
    def _():
        signal(z - 1, y, c)

    @pl.when(z < long - 1)
    def _():
        signal(z + 1, y, c)

    peers = 2 + (z > 0).astype(jnp.int32) + (z < long - 1).astype(jnp.int32)
    pl.semaphore_wait(barrier, peers)


class Gather:
    def __init__(self, long, z, y, c, views, routes, firsts, send_sem, recv_sem):
        self.long, self.z, self.y, self.c = long, z, y, c
        self.views, self.routes, self.firsts = views, routes, firsts
        self.send_sem, self.recv_sem = send_sem, recv_sem
        self.me = self.index(z, y, c)
        self.targets = (
            self.index(z + 1, y, c), self.index(z - 1, y, c),
            self.index(z, 1 - y, c), self.index(z, y, 1 - c),
        )

    def index(self, zz, yy, cc):
        return zz * 4 + yy * 2 + cc

    def copy(self, part, kind, owner, src=None):
        view = self.views[part](owner)
        return pltpu.make_async_remote_copy(
            src_ref=view if src is None else src,
            dst_ref=view,
            send_sem=self.send_sem.at[part, kind, owner],
            recv_sem=self.recv_sem.at[part, owner],
            device_id={"latent": self.targets[kind]},
            device_id_type=MESH,
        )

    def arrived(self, part, owner):
        self.copy(part, 3, owner).wait_recv()

    def sideways(self, part, owner, src=None):
        pl.when(self.z < self.long - 1)(lambda: self.copy(part, 0, owner, src).start())
        pl.when(self.z > 0)(lambda: self.copy(part, 1, owner, src).start())

    def begin(self, part):
        src = self.firsts[part]
        if self.routes[part] == 1:
            self.copy(part, 2, self.me, src).start()
            self.sideways(part, self.me, src)
        else:
            self.sideways(part, self.me, src)
            self.copy(part, 2, self.me, src).start()
        self.copy(part, 3, self.me, src).start()

    def line(self, part, step):
        z, y, c, long = self.z, self.y, self.c, self.long
        sides = (y,) if self.routes[part] == 0 else (y, 1 - y)

        def take(zz, kind, inside):
            for side in sides:
                owner = self.index(zz, side, c)
                self.arrived(part, owner)
                pl.when(inside)(lambda owner=owner: self.copy(part, kind, owner).start())
                if self.routes[part] == 0:
                    self.copy(part, 2, owner).start()
                self.copy(part, 3, owner).start()

        pl.when(z - step >= 0)(lambda: take(z - step, 0, z < long - 1))
        pl.when(z + step <= long - 1)(lambda: take(z + step, 1, z > 0))

    def across(self, part, step):
        z, y, c, long = self.z, self.y, self.c, self.long

        def take(zz):
            owner = self.index(zz, 1 - y, c)
            self.arrived(part, owner)
            if self.routes[part] == 1:
                self.sideways(part, owner)
            self.copy(part, 3, owner).start()

        if step == 0:
            take(z)
        elif self.routes[part] == 0:
            pl.when(z - step >= 0)(lambda: take(z - step))
            pl.when(z + step <= long - 1)(lambda: take(z + step))

    def finish(self, part):
        z, y, c, long = self.z, self.y, self.c, self.long
        for zz in range(long):
            for yy in range(2):
                self.arrived(part, self.index(zz, yy, 1 - c))
        for zz in range(long):
            for side in (y, 1 - y):
                owner = self.index(zz, side, c)
                self.copy(part, 3, owner).wait_send()
                if side is y or self.routes[part] == 1:
                    pl.when(jnp.logical_and(z < long - 1, zz <= z))(
                        lambda owner=owner: self.copy(part, 0, owner).wait_send()
                    )
                    pl.when(jnp.logical_and(z > 0, zz >= z))(
                        lambda owner=owner: self.copy(part, 1, owner).wait_send()
                    )
            if self.routes[part] == 0:
                self.copy(part, 2, self.index(zz, y, c)).wait_send()
        if self.routes[part] == 1:
            self.copy(part, 2, self.me).wait_send()


def column_cuts(width, share):
    cut = int(width * share) // 128 * 128
    return (pl.ds(0, cut), pl.ds(cut, width - cut))


def rows_of(owner, rows):
    return pl.ds(pl.multiple_of(owner * rows, rows), rows)


def gather_kernel(n, own_ref, whole_ref, send_sem, recv_sem, local_sem):
    long = n // 4
    layers, rows, width = own_ref.shape
    z, y, c = position()
    greet(long, z, y, c)
    cuts = column_cuts(width, 5 / 6)
    views = [
        lambda owner, cut=cut: whole_ref.at[:, rows_of(owner, rows), cut] for cut in cuts
    ]
    firsts = [own_ref.at[:, :, cut] for cut in cuts]
    gather = Gather(long, z, y, c, views, (0, 1), firsts, send_sem, recv_sem)
    local = pltpu.make_async_copy(
        own_ref, whole_ref.at[:, rows_of(gather.me, rows), :], local_sem
    )
    local.start()
    gather.begin(1)
    gather.begin(0)
    gather.across(1, 0)
    for step in range(1, long):
        gather.line(0, step)
        gather.line(1, step)
        gather.across(0, step - 1)
    gather.across(0, long - 1)
    gather.finish(0)
    gather.finish(1)
    local.wait()


def gather_rows(own, n, collective_id):
    layers, rows, width = own.shape
    return pl.pallas_call(
        functools.partial(gather_kernel, n),
        out_shape=jax.ShapeDtypeStruct((layers, n * rows, width), own.dtype),
        in_specs=[pl.BlockSpec(memory_space=pl.ANY)],
        out_specs=pl.BlockSpec(memory_space=pl.ANY),
        scratch_shapes=[
            pltpu.SemaphoreType.DMA((2, 4, n)),
            pltpu.SemaphoreType.DMA((2, n)),
            pltpu.SemaphoreType.DMA,
        ],
        compiler_params=pltpu.CompilerParams(
            collective_id=collective_id, has_side_effects=True, vmem_limit_bytes=VMEM_LIMIT
        ),
        name="gather_rows",
    )(own)


def exchange_kernel(
    n, factor, part_ref, bias_ref, wanted_ref, sum_ref, whole_ref,
    own_error, core_buf, y_out, y_in, right_out, right_in, left_out, left_in,
    core_send, core_recv, y_send, y_recv, right_send, right_recv, left_send, left_recv,
    send_sem, recv_sem, local_sem,
):
    long = n // 4
    layers, rows, width = sum_ref.shape
    z, y, c = position()
    greet(long, z, y, c)
    f32 = jnp.float32

    def index(zz, yy, cc):
        return zz * 4 + yy * 2 + cc

    def remote(src, dst, send, recv, target):
        return pltpu.make_async_remote_copy(
            src_ref=src, dst_ref=dst, send_sem=send, recv_sem=recv,
            device_id={"latent": target}, device_id_type=MESH,
        )

    order = []
    low, high = 0, long - 1
    while low <= high:
        order.append(high)
        if low < high:
            order.append(low)
        low, high = low + 1, high - 1
    pieces = [(zz, t) for t in range(layers) for zz in order]

    def core_copy(zz, side, t):
        owner = index(zz, 1 - y if side == 0 else y, 1 - c)
        return remote(
            part_ref.at[t, rows_of(owner, rows), :], core_buf.at[side, zz, t],
            core_send.at[side, zz, t], core_recv.at[side, zz, t], index(z, y, 1 - c),
        )

    def y_copy(zz, t):
        return remote(
            y_out.at[zz, t], y_in.at[zz, t], y_send.at[zz, t], y_recv.at[zz, t],
            index(z, 1 - y, c),
        )

    def right_copy(zz, t):
        return remote(
            right_out.at[zz, t], right_in.at[zz, t], right_send.at[zz, t], right_recv.at[zz, t],
            index(z + 1, y, c),
        )

    def left_copy(zz, t):
        return remote(
            left_out.at[zz, t], left_in.at[zz, t], left_send.at[zz, t], left_recv.at[zz, t],
            index(z - 1, y, c),
        )

    for zz, t in pieces:
        for side in range(2):
            core_copy(zz, side, t).start()

    def start_y(piece):
        zz, t = piece
        core_copy(zz, 0, t).wait_recv()
        owner = index(zz, 1 - y, c)
        total = part_ref[t, rows_of(owner, rows), :].astype(f32) + core_buf[0, zz, t].astype(f32)
        y_out[zz, t] = total.astype(y_out.dtype)
        y_copy(zz, t).start()

    ahead = min(3, len(pieces))

    def sum_piece(number):
        zz, t = pieces[number]
        core_copy(zz, 1, t).wait_recv()
        y_copy(zz, t).wait_recv()
        if number + ahead < len(pieces):
            start_y(pieces[number + ahead])

        def here():
            owner = index(zz, y, c)
            return (
                part_ref[t, rows_of(owner, rows), :].astype(f32)
                + core_buf[1, zz, t].astype(f32)
                + y_in[zz, t].astype(f32)
            )

        @pl.when(zz == z)
        def _():
            sum_ref[t] = here() + bias_ref[pl.ds(t, 1), :]

        @pl.when(zz > z)
        def _():
            @pl.when(z == 0)
            def _():
                right_out[zz, t] = here().astype(right_out.dtype)

            @pl.when(z > 0)
            def _():
                right_copy(zz, t).wait_recv()
                right_out[zz, t] = (here() + right_in[zz, t].astype(f32)).astype(right_out.dtype)

            right_copy(zz, t).start()

        @pl.when(zz < z)
        def _():
            @pl.when(z == long - 1)
            def _():
                left_out[zz, t] = here().astype(left_out.dtype)

            @pl.when(z < long - 1)
            def _():
                left_copy(zz, t).wait_recv()
                left_out[zz, t] = (here() + left_in[zz, t].astype(f32)).astype(left_out.dtype)

            left_copy(zz, t).start()

    cuts = column_cuts(width, 2 / 3)
    views, firsts = [], []
    for t in range(layers):
        for cut in cuts:
            views.append(
                lambda owner, t=t, cut=cut: whole_ref.at[t, rows_of(owner, rows), cut]
            )
            firsts.append(own_error.at[t, :, cut])
    gather = Gather(
        long, z, y, c, views, (0, 1) * layers, firsts, send_sem, recv_sem
    )

    def local(t):
        return pltpu.make_async_copy(
            own_error.at[t], whole_ref.at[t, rows_of(gather.me, rows), :], local_sem.at[t]
        )

    def close(t):
        @pl.when(z > 0)
        def _():
            right_copy(z, t).wait_recv()
            sum_ref[t] += right_in[z, t].astype(f32)

        @pl.when(z < long - 1)
        def _():
            left_copy(z, t).wait_recv()
            sum_ref[t] += left_in[z, t].astype(f32)

        own_error[t] = ((sum_ref[t] - wanted_ref[t].astype(f32)) * factor).astype(own_error.dtype)
        local(t).start()
        gather.begin(2 * t + 1)
        gather.begin(2 * t)

    def spread_step(t, step):
        gather.line(2 * t, step)
        if step == 1:
            gather.across(2 * t + 1, 0)
        gather.line(2 * t + 1, step)

    for piece in pieces[:ahead]:
        start_y(piece)
    for t in range(layers):
        for number in range(long):
            sum_piece(t * long + number)
            if t > 0 and number > 0:
                spread_step(t - 1, number)
        close(t)
        if t > 0:
            for step in range(long):
                gather.across(2 * (t - 1), step)
    for step in range(1, long):
        spread_step(layers - 1, step)
        gather.across(2 * (layers - 1), step - 1)
    gather.across(2 * (layers - 1), long - 1)

    for zz, t in pieces:
        core_copy(zz, 0, t).wait_send()
        core_copy(zz, 1, t).wait_send()
        y_copy(zz, t).wait_send()
        pl.when(zz > z)(lambda zz=zz, t=t: right_copy(zz, t).wait_send())
        pl.when(zz < z)(lambda zz=zz, t=t: left_copy(zz, t).wait_send())
    for t in range(layers):
        gather.finish(2 * t)
        gather.finish(2 * t + 1)
        local(t).wait()


def exchange(parts, bias, wanted, factor, n, collective_id):
    layers, all_rows, width = parts.shape
    rows, long = all_rows // n, n // 4
    line = pltpu.VMEM((long, layers, rows, width), parts.dtype)
    sems = pltpu.SemaphoreType.DMA((long, layers))
    two_sems = pltpu.SemaphoreType.DMA((2, long, layers))
    vmem = pl.BlockSpec(memory_space=pltpu.VMEM)
    return pl.pallas_call(
        functools.partial(exchange_kernel, n, factor),
        out_shape=(
            jax.ShapeDtypeStruct((layers, rows, width), jnp.float32),
            jax.ShapeDtypeStruct((layers, all_rows, width), parts.dtype),
        ),
        in_specs=[vmem, vmem, vmem],
        out_specs=(vmem, pl.BlockSpec(memory_space=pl.ANY)),
        scratch_shapes=[
            pltpu.VMEM((layers, rows, width), parts.dtype),
            pltpu.VMEM((2, long, layers, rows, width), parts.dtype),
            line, line, line, line, line, line,
            two_sems, two_sems, sems, sems, sems, sems, sems, sems,
            pltpu.SemaphoreType.DMA((2 * layers, 4, n)),
            pltpu.SemaphoreType.DMA((2 * layers, n)),
            pltpu.SemaphoreType.DMA((layers,)),
        ],
        compiler_params=pltpu.CompilerParams(
            collective_id=collective_id, has_side_effects=True, vmem_limit_bytes=VMEM_LIMIT
        ),
        name="exchange",
    )(parts, bias, wanted)


def plain_gather(own):
    return lax.all_gather(own, "latent", axis=1, tiled=True)


def body(n, row_store, row_slot, targets, enc_weight, enc_bias, dec_weight, dec_bias):
    layers = enc_weight.shape[0]
    row_count = row_slot.shape[0]
    own_rows = targets.shape[0]
    f32, bf16 = jnp.float32, jnp.bfloat16
    by_kernel = n % 4 == 0 and row_store.shape[0] % 16 == 0 and own_rows % 16 == 0

    store = jnp.transpose(row_store, (1, 0, 2))
    slots = gather_rows(store, n, 0) if by_kernel else plain_gather(store)
    slot_count = slots.shape[1]
    pick = row_slot[:, None] == jnp.arange(slot_count, dtype=row_slot.dtype)[None, :]
    slot_pre = jnp.concatenate(
        [
            jnp.dot(slots[source], enc_weight[source], preferred_element_type=f32)
            for source in range(layers)
        ],
        axis=1,
    )
    row_pre = jnp.dot(
        pick.astype(f32), slot_pre, precision=lax.Precision.HIGHEST, preferred_element_type=f32
    )
    wide = enc_weight.shape[2]
    pre_list = []
    latents = []
    for source in range(layers):
        pre_acts = row_pre[:, source * wide : (source + 1) * wide] + enc_bias[source][None, :]
        pre_list.append(pre_acts)
        latents.append(activate(pre_acts).astype(bf16))
    terms = [recon_terms(target, latents, dec_weight, layers) for target in range(layers)]
    factor = 1.0 / math.sqrt(row_count)
    wanted = jnp.transpose(targets, (1, 0, 2))
    if by_kernel:
        parts = jnp.stack([term.astype(bf16) for term in terms], axis=0)
        rebuilt, errors = exchange(parts, dec_bias, wanted, factor, n, 1)
    else:
        summed = lax.psum_scatter(
            jnp.stack(terms, axis=0), "latent", scatter_dimension=1, tiled=True
        )
        rebuilt = summed + dec_bias[:, None, :]
        errors = plain_gather(((rebuilt - wanted.astype(f32)) * factor).astype(bf16))
    grad_dec_list = []
    for source in range(layers):
        for target in range(source, layers):
            grad_dec_list.append(
                jnp.dot(latents[source].T, errors[target], preferred_element_type=f32).astype(bf16)
            )
    grad_dec = jnp.stack(grad_dec_list, axis=0)
    grad_dbias = jnp.sum(errors.astype(f32), axis=1)
    grad_ebias_list = []
    low_list = []
    for source in range(layers):
        back = None
        for target in range(source, layers):
            product = lax.dot_general(
                errors[target],
                dec_weight[pair_index(source, target, layers)],
                (((1,), (1,)), ((), ())),
                preferred_element_type=f32,
            )
            back = product if back is None else back + product
        unused, pullback = jax.vjp(activate, pre_list[source])
        dpre = pullback(back)[0]
        grad_ebias_list.append(jnp.sum(dpre, axis=0))
        low_list.append(dpre.astype(bf16))
    slot_dpre = lax.dot_general(
        pick.astype(bf16),
        jnp.concatenate(low_list, axis=1),
        (((0,), (0,)), ((), ())),
        preferred_element_type=f32,
    ).astype(bf16)
    grad_enc = jnp.stack(
        [
            lax.dot_general(
                slots[source],
                slot_dpre[:, source * wide : (source + 1) * wide],
                (((0,), (0,)), ((), ())),
                preferred_element_type=f32,
            ).astype(bf16)
            for source in range(layers)
        ],
        axis=0,
    )
    grad_ebias = jnp.stack(grad_ebias_list, axis=0)
    return (jnp.transpose(rebuilt, (1, 0, 2)), grad_enc, grad_ebias, grad_dec, grad_dbias)


def solution(mesh):
    in_specs = (
        P(("groups", "latent"), None, None),
        P("groups"),
        P(("groups", "latent"), None, None),
        P("groups", None, "latent"),
        P("groups", "latent"),
        P("groups", "latent", None),
        P("groups", None),
    )
    out_specs = (
        P(("groups", "latent"), None, None),
        P("groups", None, "latent"),
        P("groups", "latent"),
        P("groups", "latent", None),
        P("groups", None),
    )
    return jax.shard_map(
        functools.partial(body, mesh.shape["latent"]),
        mesh=mesh,
        in_specs=in_specs,
        out_specs=out_specs,
        check_vma=False,
    )
```

```python
import functools
import math

import jax
import jax.numpy as jnp
from jax import lax
from jax.experimental import pallas as pl
from jax.experimental.pallas import tpu as pltpu
from jax.sharding import PartitionSpec as P

MESH = pl.DeviceIdType.MESH
VMEM_LIMIT = 56 * 1024 * 1024


def pair_index(source, target, layers):
    return source * layers - source * (source - 1) // 2 + target - source


def activate(values):
    return jax.nn.gelu(values, approximate=True)


def position():
    me = lax.axis_index("latent")
    return me // 4, (me // 2) % 2, me % 2


def greet(long, z, y, c):
    barrier = pltpu.get_barrier_semaphore()

    def signal(zz, yy, cc):
        pl.semaphore_signal(
            barrier, inc=1, device_id={"latent": zz * 4 + yy * 2 + cc}, device_id_type=MESH
        )

    signal(z, y, 1 - c)
    signal(z, 1 - y, c)

    @pl.when(z > 0)
    def _():
        signal(z - 1, y, c)

    @pl.when(z < long - 1)
    def _():
        signal(z + 1, y, c)

    peers = 2 + (z > 0).astype(jnp.int32) + (z < long - 1).astype(jnp.int32)
    pl.semaphore_wait(barrier, peers)


class Gather:
    def __init__(self, long, z, y, c, views, routes, firsts, send_sem, recv_sem):
        self.long, self.z, self.y, self.c = long, z, y, c
        self.views, self.routes, self.firsts = views, routes, firsts
        self.send_sem, self.recv_sem = send_sem, recv_sem
        self.me = self.index(z, y, c)
        self.targets = (
            self.index(z + 1, y, c), self.index(z - 1, y, c),
            self.index(z, 1 - y, c), self.index(z, y, 1 - c),
        )

    def index(self, zz, yy, cc):
        return zz * 4 + yy * 2 + cc

    def copy(self, part, kind, owner, src=None):
        view = self.views[part](owner)
        return pltpu.make_async_remote_copy(
            src_ref=view if src is None else src,
            dst_ref=view,
            send_sem=self.send_sem.at[part, kind, owner],
            recv_sem=self.recv_sem.at[part, owner],
            device_id={"latent": self.targets[kind]},
            device_id_type=MESH,
        )

    def arrived(self, part, owner):
        self.copy(part, 3, owner).wait_recv()

    def sideways(self, part, owner, src=None):
        pl.when(self.z < self.long - 1)(lambda: self.copy(part, 0, owner, src).start())
        pl.when(self.z > 0)(lambda: self.copy(part, 1, owner, src).start())

    def begin(self, part):
        src = self.firsts[part]
        if self.routes[part] == 1:
            self.copy(part, 2, self.me, src).start()
            self.sideways(part, self.me, src)
        else:
            self.sideways(part, self.me, src)
            self.copy(part, 2, self.me, src).start()
        self.copy(part, 3, self.me, src).start()

    def line(self, part, step):
        z, y, c, long = self.z, self.y, self.c, self.long
        sides = (y,) if self.routes[part] == 0 else (y, 1 - y)

        def take(zz, kind, inside):
            for side in sides:
                owner = self.index(zz, side, c)
                self.arrived(part, owner)
                pl.when(inside)(lambda owner=owner: self.copy(part, kind, owner).start())
                if self.routes[part] == 0:
                    self.copy(part, 2, owner).start()
                self.copy(part, 3, owner).start()

        pl.when(z - step >= 0)(lambda: take(z - step, 0, z < long - 1))
        pl.when(z + step <= long - 1)(lambda: take(z + step, 1, z > 0))

    def across(self, part, step):
        z, y, c, long = self.z, self.y, self.c, self.long

        def take(zz):
            owner = self.index(zz, 1 - y, c)
            self.arrived(part, owner)
            if self.routes[part] == 1:
                self.sideways(part, owner)
            self.copy(part, 3, owner).start()

        if step == 0:
            take(z)
        elif self.routes[part] == 0:
            pl.when(z - step >= 0)(lambda: take(z - step))
            pl.when(z + step <= long - 1)(lambda: take(z + step))

    def finish(self, part):
        z, y, c, long = self.z, self.y, self.c, self.long
        for zz in range(long):
            for yy in range(2):
                self.arrived(part, self.index(zz, yy, 1 - c))
        for zz in range(long):
            for side in (y, 1 - y):
                owner = self.index(zz, side, c)
                self.copy(part, 3, owner).wait_send()
                if side is y or self.routes[part] == 1:
                    pl.when(jnp.logical_and(z < long - 1, zz <= z))(
                        lambda owner=owner: self.copy(part, 0, owner).wait_send()
                    )
                    pl.when(jnp.logical_and(z > 0, zz >= z))(
                        lambda owner=owner: self.copy(part, 1, owner).wait_send()
                    )
            if self.routes[part] == 0:
                self.copy(part, 2, self.index(zz, y, c)).wait_send()
        if self.routes[part] == 1:
            self.copy(part, 2, self.me).wait_send()


def column_cuts(width, share):
    cut = int(width * share) // 128 * 128
    return (pl.ds(0, cut), pl.ds(cut, width - cut))


def rows_of(owner, rows):
    return pl.ds(pl.multiple_of(owner * rows, rows), rows)


def gather_kernel(n, own_ref, whole_ref, send_sem, recv_sem, local_sem):
    long = n // 4
    layers, rows, width = own_ref.shape
    z, y, c = position()
    greet(long, z, y, c)
    cuts = column_cuts(width, 5 / 6)
    views = [
        lambda owner, cut=cut: whole_ref.at[:, rows_of(owner, rows), cut] for cut in cuts
    ]
    firsts = [own_ref.at[:, :, cut] for cut in cuts]
    gather = Gather(long, z, y, c, views, (0, 1), firsts, send_sem, recv_sem)
    local = pltpu.make_async_copy(
        own_ref, whole_ref.at[:, rows_of(gather.me, rows), :], local_sem
    )
    local.start()
    gather.begin(1)
    gather.begin(0)
    gather.across(1, 0)
    for step in range(1, long):
        gather.line(0, step)
        gather.line(1, step)
        gather.across(0, step - 1)
    gather.across(0, long - 1)
    gather.finish(0)
    gather.finish(1)
    local.wait()


def gather_rows(own, n, collective_id):
    layers, rows, width = own.shape
    return pl.pallas_call(
        functools.partial(gather_kernel, n),
        out_shape=jax.ShapeDtypeStruct((layers, n * rows, width), own.dtype),
        in_specs=[pl.BlockSpec(memory_space=pl.ANY)],
        out_specs=pl.BlockSpec(memory_space=pl.ANY),
        scratch_shapes=[
            pltpu.SemaphoreType.DMA((2, 4, n)),
            pltpu.SemaphoreType.DMA((2, n)),
            pltpu.SemaphoreType.DMA,
        ],
        compiler_params=pltpu.CompilerParams(
            collective_id=collective_id, has_side_effects=True, vmem_limit_bytes=VMEM_LIMIT
        ),
        name=f"gather_rows_{rows}",
    )(own)


def scatter_kernel(
    n, part_ref, sum_ref, core_buf, y_out, y_in, right_out, right_in, left_out, left_in,
    core_send, core_recv, y_send, y_recv, right_send, right_recv, left_send, left_recv,
):
    long = n // 4
    layers, rows, width = sum_ref.shape
    z, y, c = position()
    greet(long, z, y, c)
    f32 = jnp.float32

    def index(zz, yy, cc):
        return zz * 4 + yy * 2 + cc

    def own_rows(owner):
        return rows_of(owner, rows)

    def remote(src, dst, send, recv, target):
        return pltpu.make_async_remote_copy(
            src_ref=src, dst_ref=dst, send_sem=send, recv_sem=recv,
            device_id={"latent": target}, device_id_type=MESH,
        )

    order = []
    low, high = 0, long - 1
    while low <= high:
        order.append(high)
        if low < high:
            order.append(low)
        low, high = low + 1, high - 1
    pieces = [(zz, t) for zz in order for t in range(layers)]

    def core_copy(zz, side, t):
        owner = index(zz, 1 - y if side == 0 else y, 1 - c)
        return remote(
            part_ref.at[t, own_rows(owner), :], core_buf.at[side, zz, t],
            core_send.at[side, zz, t], core_recv.at[side, zz, t], index(z, y, 1 - c),
        )

    def y_copy(zz, t):
        return remote(
            y_out.at[zz, t], y_in.at[zz, t], y_send.at[zz, t], y_recv.at[zz, t],
            index(z, 1 - y, c),
        )

    def right_copy(zz, t):
        return remote(
            right_out.at[zz, t], right_in.at[zz, t], right_send.at[zz, t], right_recv.at[zz, t],
            index(z + 1, y, c),
        )

    def left_copy(zz, t):
        return remote(
            left_out.at[zz, t], left_in.at[zz, t], left_send.at[zz, t], left_recv.at[zz, t],
            index(z - 1, y, c),
        )

    for side in range(2):
        for zz, t in pieces:
            core_copy(zz, side, t).start()

    def start_y(piece):
        zz, t = piece
        core_copy(zz, 0, t).wait_recv()
        owner = index(zz, 1 - y, c)
        total = part_ref[t, own_rows(owner), :].astype(f32) + core_buf[0, zz, t].astype(f32)
        y_out[zz, t] = total.astype(y_out.dtype)
        y_copy(zz, t).start()

    ahead = 2
    for piece in pieces[:ahead]:
        start_y(piece)
    for number, (zz, t) in enumerate(pieces):
        core_copy(zz, 1, t).wait_recv()
        y_copy(zz, t).wait_recv()
        if number + ahead < len(pieces):
            start_y(pieces[number + ahead])

        def here(zz=zz, t=t):
            owner = index(zz, y, c)
            return (
                part_ref[t, own_rows(owner), :].astype(f32)
                + core_buf[1, zz, t].astype(f32)
                + y_in[zz, t].astype(f32)
            )

        @pl.when(zz == z)
        def _():
            sum_ref[t] = here()

        @pl.when(zz > z)
        def _():
            @pl.when(z == 0)
            def _():
                right_out[zz, t] = here().astype(right_out.dtype)

            @pl.when(z > 0)
            def _():
                right_copy(zz, t).wait_recv()
                right_out[zz, t] = (here() + right_in[zz, t].astype(f32)).astype(right_out.dtype)

            right_copy(zz, t).start()

        @pl.when(zz < z)
        def _():
            @pl.when(z == long - 1)
            def _():
                left_out[zz, t] = here().astype(left_out.dtype)

            @pl.when(z < long - 1)
            def _():
                left_copy(zz, t).wait_recv()
                left_out[zz, t] = (here() + left_in[zz, t].astype(f32)).astype(left_out.dtype)

            left_copy(zz, t).start()

    for t in range(layers):
        @pl.when(z > 0)
        def _():
            right_copy(z, t).wait_recv()
            sum_ref[t] += right_in[z, t].astype(f32)

        @pl.when(z < long - 1)
        def _():
            left_copy(z, t).wait_recv()
            sum_ref[t] += left_in[z, t].astype(f32)

    for zz, t in pieces:
        core_copy(zz, 0, t).wait_send()
        core_copy(zz, 1, t).wait_send()
        y_copy(zz, t).wait_send()
        pl.when(zz > z)(lambda zz=zz, t=t: right_copy(zz, t).wait_send())
        pl.when(zz < z)(lambda zz=zz, t=t: left_copy(zz, t).wait_send())


def scatter_sum(parts, n, collective_id):
    layers, all_rows, width = parts.shape
    rows, long = all_rows // n, n // 4
    line = pltpu.VMEM((long, layers, rows, width), parts.dtype)
    sems = pltpu.SemaphoreType.DMA((long, layers))
    two_sems = pltpu.SemaphoreType.DMA((2, long, layers))
    return pl.pallas_call(
        functools.partial(scatter_kernel, n),
        out_shape=jax.ShapeDtypeStruct((layers, rows, width), jnp.float32),
        in_specs=[pl.BlockSpec(memory_space=pltpu.VMEM)],
        out_specs=pl.BlockSpec(memory_space=pltpu.VMEM),
        scratch_shapes=[
            pltpu.VMEM((2, long, layers, rows, width), parts.dtype),
            line, line, line, line, line, line,
            two_sems, two_sems, sems, sems, sems, sems, sems, sems,
        ],
        compiler_params=pltpu.CompilerParams(
            collective_id=collective_id, has_side_effects=True, vmem_limit_bytes=VMEM_LIMIT
        ),
        name="scatter_sum",
    )(parts)


def front_kernel(
    tiles, slot_ref, slots_ref, enc_ref, ebias_ref, dec_ref, pre_ref, latent_ref, part_ref, total
):
    step = pl.program_id(0)
    f32, bf16 = jnp.float32, jnp.bfloat16
    layers, slot_count, _ = slots_ref.shape

    @pl.when(step == 0)
    def _():
        total[...] = jnp.zeros_like(total)

    @pl.when(step < tiles)
    def _():
        for source in range(layers):
            total[source] += jnp.dot(
                slots_ref[source], enc_ref[source], preferred_element_type=f32
            )

    @pl.when(step == tiles - 1)
    def _():
        shape = (slot_ref.shape[0], slot_count)
        pick = (slot_ref[...] == lax.broadcasted_iota(jnp.int32, shape, 1)).astype(f32)
        pick = pick.astype(bf16)
        for source in range(layers):
            rest = total[source]
            row_pre = None
            for _ in range(3):
                term = rest.astype(bf16)
                rest = rest - term.astype(f32)
                product = jnp.dot(pick, term, preferred_element_type=f32)
                row_pre = product if row_pre is None else row_pre + product
            pre_acts = row_pre + ebias_ref[pl.ds(source, 1), :]
            pre_ref[source] = pre_acts
            latent_ref[source] = activate(pre_acts).astype(bf16)

    @pl.when(step >= tiles)
    def _():
        for target in range(layers):
            summed = None
            for source in range(target + 1):
                product = jnp.dot(
                    latent_ref[source],
                    dec_ref[pair_index(source, target, layers)],
                    preferred_element_type=f32,
                )
                summed = product if summed is None else summed + product
            part_ref[target] = summed.astype(part_ref.dtype)


def tile_of(width):
    return 512 if width % 512 == 0 else width


def front(row_slot, slots, enc_weight, enc_bias, dec_weight, part_dtype):
    layers, slot_count, width = slots.shape
    pairs, wide, _ = dec_weight.shape
    row_count = row_slot.shape[0]
    tile = tile_of(width)
    tiles = width // tile

    def early(step):
        return jnp.minimum(step, tiles - 1)

    def late(step):
        return jnp.maximum(step - tiles, 0)

    return pl.pallas_call(
        functools.partial(front_kernel, tiles),
        grid=(2 * tiles,),
        out_shape=(
            jax.ShapeDtypeStruct((layers, row_count, wide), jnp.float32),
            jax.ShapeDtypeStruct((layers, row_count, wide), jnp.bfloat16),
            jax.ShapeDtypeStruct((layers, row_count, width), part_dtype),
        ),
        in_specs=[
            pl.BlockSpec((row_count, 1), lambda i: (0, 0)),
            pl.BlockSpec((layers, slot_count, tile), lambda i: (0, 0, early(i))),
            pl.BlockSpec((layers, tile, wide), lambda i: (0, early(i), 0)),
            pl.BlockSpec((layers, wide), lambda i: (0, 0)),
            pl.BlockSpec((pairs, wide, tile), lambda i: (0, 0, late(i))),
        ],
        out_specs=(
            pl.BlockSpec((layers, row_count, wide), lambda i: (0, 0, 0)),
            pl.BlockSpec((layers, row_count, wide), lambda i: (0, 0, 0)),
            pl.BlockSpec((layers, row_count, tile), lambda i: (0, 0, late(i))),
        ),
        scratch_shapes=[pltpu.VMEM((layers, slot_count, wide), jnp.float32)],
        compiler_params=pltpu.CompilerParams(vmem_limit_bytes=VMEM_LIMIT),
        name="front",
    )(row_slot[:, None], slots, enc_weight, enc_bias, dec_weight)


def tail_kernel(
    tiles, slot_ref, pre_ref, latent_ref, errors_ref, dec_ref, slots_ref,
    gdec_ref, gdbias_ref, gebias_ref, genc_ref, back, spread,
):
    step = pl.program_id(0)
    f32, bf16 = jnp.float32, jnp.bfloat16
    layers, slot_count, _ = slots_ref.shape
    over_rows = (((0,), (0,)), ((), ()))
    over_width = (((1,), (1,)), ((), ()))

    @pl.when(step == 0)
    def _():
        back[...] = jnp.zeros_like(back)

    @pl.when(step < tiles)
    def _():
        for target in range(layers):
            error = errors_ref[target]
            gdbias_ref[pl.ds(target, 1), :] = jnp.sum(error.astype(f32), axis=0, keepdims=True)
            for source in range(target + 1):
                pair = pair_index(source, target, layers)
                gdec_ref[pair] = lax.dot_general(
                    latent_ref[source], error, over_rows, preferred_element_type=f32
                ).astype(gdec_ref.dtype)
                back[source] += lax.dot_general(
                    error, dec_ref[pair], over_width, preferred_element_type=f32
                )

    @pl.when(step == tiles - 1)
    def _():
        shape = (slot_count, slot_ref.shape[1])
        place = (slot_ref[...] == lax.broadcasted_iota(jnp.int32, shape, 0)).astype(f32)
        place = place.astype(bf16)
        for source in range(layers):
            unused, pullback = jax.vjp(activate, pre_ref[source])
            dpre = pullback(back[source])[0]
            gebias_ref[pl.ds(source, 1), :] = jnp.sum(dpre, axis=0, keepdims=True)
            spread[source] = jnp.dot(
                place, dpre.astype(bf16), preferred_element_type=f32
            ).astype(bf16)

    @pl.when(step >= tiles)
    def _():
        for source in range(layers):
            genc_ref[source] = lax.dot_general(
                slots_ref[source], spread[source], over_rows, preferred_element_type=f32
            ).astype(genc_ref.dtype)


def tail(row_slot, pre, latents, errors, dec_weight, slots):
    layers, slot_count, width = slots.shape
    pairs, wide, _ = dec_weight.shape
    row_count = row_slot.shape[0]
    tile = tile_of(width)
    tiles = width // tile
    bf16 = jnp.bfloat16

    def early(step):
        return jnp.minimum(step, tiles - 1)

    def late(step):
        return jnp.maximum(step - tiles, 0)

    return pl.pallas_call(
        functools.partial(tail_kernel, tiles),
        grid=(2 * tiles,),
        out_shape=(
            jax.ShapeDtypeStruct((pairs, wide, width), bf16),
            jax.ShapeDtypeStruct((layers, width), jnp.float32),
            jax.ShapeDtypeStruct((layers, wide), jnp.float32),
            jax.ShapeDtypeStruct((layers, width, wide), bf16),
        ),
        in_specs=[
            pl.BlockSpec((1, row_count), lambda i: (0, 0)),
            pl.BlockSpec((layers, row_count, wide), lambda i: (0, 0, 0)),
            pl.BlockSpec((layers, row_count, wide), lambda i: (0, 0, 0)),
            pl.BlockSpec((layers, row_count, tile), lambda i: (0, 0, early(i))),
            pl.BlockSpec((pairs, wide, tile), lambda i: (0, 0, early(i))),
            pl.BlockSpec((layers, slot_count, tile), lambda i: (0, 0, late(i))),
        ],
        out_specs=(
            pl.BlockSpec((pairs, wide, tile), lambda i: (0, 0, early(i))),
            pl.BlockSpec((layers, tile), lambda i: (0, early(i))),
            pl.BlockSpec((layers, wide), lambda i: (0, 0)),
            pl.BlockSpec((layers, tile, wide), lambda i: (0, late(i), 0)),
        ),
        scratch_shapes=[
            pltpu.VMEM((layers, row_count, wide), jnp.float32),
            pltpu.VMEM((layers, slot_count, wide), bf16),
        ],
        compiler_params=pltpu.CompilerParams(vmem_limit_bytes=VMEM_LIMIT),
        name="tail",
    )(row_slot[None, :], pre, latents, errors, dec_weight, slots)


def plain_gather(own):
    return lax.all_gather(own, "latent", axis=1, tiled=True)


def body(n, row_store, row_slot, targets, enc_weight, enc_bias, dec_weight, dec_bias):
    layers = enc_weight.shape[0]
    row_count = row_slot.shape[0]
    own_rows = targets.shape[0]
    f32, bf16 = jnp.float32, jnp.bfloat16
    by_kernel = n % 4 == 0 and row_store.shape[0] % 16 == 0 and own_rows % 16 == 0

    store = jnp.transpose(row_store, (1, 0, 2))
    slots = gather_rows(store, n, 0) if by_kernel else plain_gather(store)
    pre, latents, parts = front(
        row_slot, slots, enc_weight, enc_bias, dec_weight, bf16 if by_kernel else f32
    )
    if by_kernel:
        summed = scatter_sum(parts, n, 1)
    else:
        summed = lax.psum_scatter(parts, "latent", scatter_dimension=1, tiled=True)
    rebuilt = summed + dec_bias[:, None, :]
    factor = 1.0 / math.sqrt(row_count)
    wanted = jnp.transpose(targets, (1, 0, 2)).astype(f32)
    error_part = ((rebuilt - wanted) * factor).astype(bf16)
    errors = gather_rows(error_part, n, 2) if by_kernel else plain_gather(error_part)
    grad_dec, grad_dbias, grad_ebias, grad_enc = tail(
        row_slot, pre, latents, errors, dec_weight, slots
    )
    return (jnp.transpose(rebuilt, (1, 0, 2)), grad_enc, grad_ebias, grad_dec, grad_dbias)


def solution(mesh):
    in_specs = (
        P(("groups", "latent"), None, None),
        P("groups"),
        P(("groups", "latent"), None, None),
        P("groups", None, "latent"),
        P("groups", "latent"),
        P("groups", "latent", None),
        P("groups", None),
    )
    out_specs = (
        P(("groups", "latent"), None, None),
        P("groups", None, "latent"),
        P("groups", "latent"),
        P("groups", "latent", None),
        P("groups", None),
    )
    return jax.shard_map(
        functools.partial(body, mesh.shape["latent"]),
        mesh=mesh,
        in_specs=in_specs,
        out_specs=out_specs,
        check_vma=False,
    )
```

```python
import functools
import math

import jax
import jax.numpy as jnp
from jax import lax
from jax.experimental import pallas as pl
from jax.experimental.pallas import tpu as pltpu
from jax.sharding import PartitionSpec as P

MESH = pl.DeviceIdType.MESH
VMEM_LIMIT = 56 * 1024 * 1024


def pair_index(source, target, layers):
    return source * layers - source * (source - 1) // 2 + target - source


def activate(values):
    return jax.nn.gelu(values, approximate=True)


def recon_terms(target, latents, dec_weight, layers):
    summed_terms = None
    for source in range(target + 1):
        product = jnp.dot(
            latents[source],
            dec_weight[pair_index(source, target, layers)],
            preferred_element_type=jnp.float32,
        )
        summed_terms = product if summed_terms is None else summed_terms + product
    return summed_terms


def position():
    me = lax.axis_index("latent")
    return me // 4, (me // 2) % 2, me % 2


def greet(long, z, y, c):
    barrier = pltpu.get_barrier_semaphore()

    def signal(zz, yy, cc):
        pl.semaphore_signal(
            barrier, inc=1, device_id={"latent": zz * 4 + yy * 2 + cc}, device_id_type=MESH
        )

    signal(z, y, 1 - c)
    signal(z, 1 - y, c)

    @pl.when(z > 0)
    def _():
        signal(z - 1, y, c)

    @pl.when(z < long - 1)
    def _():
        signal(z + 1, y, c)

    peers = 2 + (z > 0).astype(jnp.int32) + (z < long - 1).astype(jnp.int32)
    pl.semaphore_wait(barrier, peers)


class Gather:
    def __init__(self, long, z, y, c, views, routes, firsts, send_sem, recv_sem):
        self.long, self.z, self.y, self.c = long, z, y, c
        self.views, self.routes, self.firsts = views, routes, firsts
        self.send_sem, self.recv_sem = send_sem, recv_sem
        self.me = self.index(z, y, c)
        self.targets = (
            self.index(z + 1, y, c), self.index(z - 1, y, c),
            self.index(z, 1 - y, c), self.index(z, y, 1 - c),
        )

    def index(self, zz, yy, cc):
        return zz * 4 + yy * 2 + cc

    def copy(self, part, kind, owner, src=None):
        view = self.views[part](owner)
        return pltpu.make_async_remote_copy(
            src_ref=view if src is None else src,
            dst_ref=view,
            send_sem=self.send_sem.at[part, kind, owner],
            recv_sem=self.recv_sem.at[part, owner],
            device_id={"latent": self.targets[kind]},
            device_id_type=MESH,
        )

    def arrived(self, part, owner):
        self.copy(part, 3, owner).wait_recv()

    def sideways(self, part, owner, src=None):
        pl.when(self.z < self.long - 1)(lambda: self.copy(part, 0, owner, src).start())
        pl.when(self.z > 0)(lambda: self.copy(part, 1, owner, src).start())

    def begin(self, part):
        src = self.firsts[part]
        if self.routes[part] == 1:
            self.copy(part, 2, self.me, src).start()
            self.sideways(part, self.me, src)
        else:
            self.sideways(part, self.me, src)
            self.copy(part, 2, self.me, src).start()
        self.copy(part, 3, self.me, src).start()

    def line(self, part, step):
        z, y, c, long = self.z, self.y, self.c, self.long
        sides = (y,) if self.routes[part] == 0 else (y, 1 - y)

        def take(zz, kind, inside):
            for side in sides:
                owner = self.index(zz, side, c)
                self.arrived(part, owner)
                pl.when(inside)(lambda owner=owner: self.copy(part, kind, owner).start())
                if self.routes[part] == 0:
                    self.copy(part, 2, owner).start()
                self.copy(part, 3, owner).start()

        pl.when(z - step >= 0)(lambda: take(z - step, 0, z < long - 1))
        pl.when(z + step <= long - 1)(lambda: take(z + step, 1, z > 0))

    def across(self, part, step):
        z, y, c, long = self.z, self.y, self.c, self.long

        def take(zz):
            owner = self.index(zz, 1 - y, c)
            self.arrived(part, owner)
            if self.routes[part] == 1:
                self.sideways(part, owner)
            self.copy(part, 3, owner).start()

        if step == 0:
            take(z)
        elif self.routes[part] == 0:
            pl.when(z - step >= 0)(lambda: take(z - step))
            pl.when(z + step <= long - 1)(lambda: take(z + step))

    def finish(self, part):
        z, y, c, long = self.z, self.y, self.c, self.long
        for zz in range(long):
            for yy in range(2):
                self.arrived(part, self.index(zz, yy, 1 - c))
        for zz in range(long):
            for side in (y, 1 - y):
                owner = self.index(zz, side, c)
                self.copy(part, 3, owner).wait_send()
                if side is y or self.routes[part] == 1:
                    pl.when(jnp.logical_and(z < long - 1, zz <= z))(
                        lambda owner=owner: self.copy(part, 0, owner).wait_send()
                    )
                    pl.when(jnp.logical_and(z > 0, zz >= z))(
                        lambda owner=owner: self.copy(part, 1, owner).wait_send()
                    )
            if self.routes[part] == 0:
                self.copy(part, 2, self.index(zz, y, c)).wait_send()
        if self.routes[part] == 1:
            self.copy(part, 2, self.me).wait_send()


def rows_of(owner, rows):
    return pl.ds(pl.multiple_of(owner * rows, rows), rows)


def gather_kernel(n, share, own_ref, whole_ref, send_sem, recv_sem, local_sem):
    long = n // 4
    layers, rows, width = own_ref.shape
    z, y, c = position()
    greet(long, z, y, c)
    cut = int(width * share) // 128 * 128
    cuts = [pl.ds(0, cut)] if cut == width else [pl.ds(0, cut), pl.ds(cut, width - cut)]
    views, firsts, routes = [], [], []
    for t in range(layers):
        for route, columns in enumerate(cuts):
            views.append(
                lambda owner, t=t, columns=columns: whole_ref.at[t, rows_of(owner, rows), columns]
            )
            firsts.append(own_ref.at[t, :, columns])
            routes.append(route)
    gather = Gather(long, z, y, c, views, routes, firsts, send_sem, recv_sem)
    local = pltpu.make_async_copy(
        own_ref, whole_ref.at[:, rows_of(gather.me, rows), :], local_sem
    )
    local.start()
    straight = [part for part, route in enumerate(routes) if route == 0]
    turned = [part for part, route in enumerate(routes) if route == 1]
    for part in turned + straight:
        gather.begin(part)
    for part in turned:
        gather.across(part, 0)
    for step in range(1, long):
        for part in straight + turned:
            gather.line(part, step)
        for part in straight:
            gather.across(part, step - 1)
    for part in straight:
        gather.across(part, long - 1)
    for part in straight + turned:
        gather.finish(part)
    local.wait()


def gather_rows(own, n, share, collective_id):
    layers, rows, width = own.shape
    parts = layers if share == 1 else 2 * layers
    return pl.pallas_call(
        functools.partial(gather_kernel, n, share),
        out_shape=jax.ShapeDtypeStruct((layers, n * rows, width), own.dtype),
        in_specs=[pl.BlockSpec(memory_space=pl.ANY)],
        out_specs=pl.BlockSpec(memory_space=pl.ANY),
        scratch_shapes=[
            pltpu.SemaphoreType.DMA((parts, 4, n)),
            pltpu.SemaphoreType.DMA((parts, n)),
            pltpu.SemaphoreType.DMA,
        ],
        compiler_params=pltpu.CompilerParams(
            collective_id=collective_id, has_side_effects=True, vmem_limit_bytes=VMEM_LIMIT
        ),
        name=f"gather_rows_{rows}",
    )(own)


def scatter_kernel(
    n, part_ref, sum_ref, core_buf, y_out, y_in, right_out, right_in, left_out, left_in,
    core_send, core_recv, y_send, y_recv, right_send, right_recv, left_send, left_recv,
):
    long = n // 4
    layers, rows, width = sum_ref.shape
    z, y, c = position()
    greet(long, z, y, c)
    f32 = jnp.float32

    def index(zz, yy, cc):
        return zz * 4 + yy * 2 + cc

    def own_rows(owner):
        return rows_of(owner, rows)

    def remote(src, dst, send, recv, target):
        return pltpu.make_async_remote_copy(
            src_ref=src, dst_ref=dst, send_sem=send, recv_sem=recv,
            device_id={"latent": target}, device_id_type=MESH,
        )

    order = []
    low, high = 0, long - 1
    while low <= high:
        order.append(high)
        if low < high:
            order.append(low)
        low, high = low + 1, high - 1
    pieces = [(zz, t) for zz in order for t in range(layers)]

    def core_copy(zz, side, t):
        owner = index(zz, 1 - y if side == 0 else y, 1 - c)
        return remote(
            part_ref.at[t, own_rows(owner), :], core_buf.at[side, zz, t],
            core_send.at[side, zz, t], core_recv.at[side, zz, t], index(z, y, 1 - c),
        )

    def y_copy(zz, t):
        return remote(
            y_out.at[zz, t], y_in.at[zz, t], y_send.at[zz, t], y_recv.at[zz, t],
            index(z, 1 - y, c),
        )

    def right_copy(zz, t):
        return remote(
            right_out.at[zz, t], right_in.at[zz, t], right_send.at[zz, t], right_recv.at[zz, t],
            index(z + 1, y, c),
        )

    def left_copy(zz, t):
        return remote(
            left_out.at[zz, t], left_in.at[zz, t], left_send.at[zz, t], left_recv.at[zz, t],
            index(z - 1, y, c),
        )

    for side in range(2):
        for zz, t in pieces:
            core_copy(zz, side, t).start()

    def start_y(piece):
        zz, t = piece
        core_copy(zz, 0, t).wait_recv()
        owner = index(zz, 1 - y, c)
        total = part_ref[t, own_rows(owner), :].astype(f32) + core_buf[0, zz, t].astype(f32)
        y_out[zz, t] = total.astype(y_out.dtype)
        y_copy(zz, t).start()

    ahead = 2
    for piece in pieces[:ahead]:
        start_y(piece)
    for number, (zz, t) in enumerate(pieces):
        core_copy(zz, 1, t).wait_recv()
        y_copy(zz, t).wait_recv()
        if number + ahead < len(pieces):
            start_y(pieces[number + ahead])

        def here(zz=zz, t=t):
            owner = index(zz, y, c)
            return (
                part_ref[t, own_rows(owner), :].astype(f32)
                + core_buf[1, zz, t].astype(f32)
                + y_in[zz, t].astype(f32)
            )

        @pl.when(zz == z)
        def _():
            sum_ref[t] = here()

        @pl.when(zz > z)
        def _():
            @pl.when(z == 0)
            def _():
                right_out[zz, t] = here().astype(right_out.dtype)

            @pl.when(z > 0)
            def _():
                right_copy(zz, t).wait_recv()
                right_out[zz, t] = (here() + right_in[zz, t].astype(f32)).astype(right_out.dtype)

            right_copy(zz, t).start()

        @pl.when(zz < z)
        def _():
            @pl.when(z == long - 1)
            def _():
                left_out[zz, t] = here().astype(left_out.dtype)

            @pl.when(z < long - 1)
            def _():
                left_copy(zz, t).wait_recv()
                left_out[zz, t] = (here() + left_in[zz, t].astype(f32)).astype(left_out.dtype)

            left_copy(zz, t).start()

    for t in range(layers):
        @pl.when(z > 0)
        def _():
            right_copy(z, t).wait_recv()
            sum_ref[t] += right_in[z, t].astype(f32)

        @pl.when(z < long - 1)
        def _():
            left_copy(z, t).wait_recv()
            sum_ref[t] += left_in[z, t].astype(f32)

    for zz, t in pieces:
        core_copy(zz, 0, t).wait_send()
        core_copy(zz, 1, t).wait_send()
        y_copy(zz, t).wait_send()
        pl.when(zz > z)(lambda zz=zz, t=t: right_copy(zz, t).wait_send())
        pl.when(zz < z)(lambda zz=zz, t=t: left_copy(zz, t).wait_send())


def scatter_sum(parts, n, collective_id):
    layers, all_rows, width = parts.shape
    rows, long = all_rows // n, n // 4
    line = pltpu.VMEM((long, layers, rows, width), parts.dtype)
    sems = pltpu.SemaphoreType.DMA((long, layers))
    two_sems = pltpu.SemaphoreType.DMA((2, long, layers))
    return pl.pallas_call(
        functools.partial(scatter_kernel, n),
        out_shape=jax.ShapeDtypeStruct((layers, rows, width), jnp.float32),
        in_specs=[pl.BlockSpec(memory_space=pltpu.VMEM)],
        out_specs=pl.BlockSpec(memory_space=pltpu.VMEM),
        scratch_shapes=[
            pltpu.VMEM((2, long, layers, rows, width), parts.dtype),
            line, line, line, line, line, line,
            two_sems, two_sems, sems, sems, sems, sems, sems, sems,
        ],
        compiler_params=pltpu.CompilerParams(
            collective_id=collective_id, has_side_effects=True, vmem_limit_bytes=VMEM_LIMIT
        ),
        name="scatter_sum",
    )(parts)


def plain_gather(own):
    return lax.all_gather(own, "latent", axis=1, tiled=True)


def body(n, row_store, row_slot, targets, enc_weight, enc_bias, dec_weight, dec_bias):
    layers = enc_weight.shape[0]
    row_count = row_slot.shape[0]
    own_rows = targets.shape[0]
    f32, bf16 = jnp.float32, jnp.bfloat16
    by_kernel = n % 4 == 0 and row_store.shape[0] % 16 == 0 and own_rows % 16 == 0

    store = jnp.transpose(row_store, (1, 0, 2))
    slots = gather_rows(store, n, 5 / 6, 0) if by_kernel else plain_gather(store)
    slot_count = slots.shape[1]
    pick = row_slot[:, None] == jnp.arange(slot_count, dtype=row_slot.dtype)[None, :]
    slot_pre = jnp.concatenate(
        [
            jnp.dot(slots[source], enc_weight[source], preferred_element_type=f32)
            for source in range(layers)
        ],
        axis=1,
    )
    row_pre = jnp.dot(
        pick.astype(f32), slot_pre, precision=lax.Precision.HIGHEST, preferred_element_type=f32
    )
    wide = enc_weight.shape[2]
    pre_list = []
    latents = []
    for source in range(layers):
        pre_acts = row_pre[:, source * wide : (source + 1) * wide] + enc_bias[source][None, :]
        pre_list.append(pre_acts)
        latents.append(activate(pre_acts).astype(bf16))
    terms = [recon_terms(target, latents, dec_weight, layers) for target in range(layers)]
    if by_kernel:
        summed = scatter_sum(jnp.stack([term.astype(bf16) for term in terms], axis=0), n, 1)
    else:
        summed = lax.psum_scatter(
            jnp.stack(terms, axis=0), "latent", scatter_dimension=1, tiled=True
        )
    rebuilt = summed + dec_bias[:, None, :]
    factor = 1.0 / math.sqrt(row_count)
    wanted = jnp.transpose(targets, (1, 0, 2)).astype(f32)
    error_part = ((rebuilt - wanted) * factor).astype(bf16)
    errors = gather_rows(error_part, n, 1, 2) if by_kernel else plain_gather(error_part)
    grad_dec_list = []
    for source in range(layers):
        for target in range(source, layers):
            grad_dec_list.append(
                jnp.dot(latents[source].T, errors[target], preferred_element_type=f32).astype(bf16)
            )
    grad_dec = jnp.stack(grad_dec_list, axis=0)
    grad_dbias = jnp.sum(errors.astype(f32), axis=1)
    grad_ebias_list = []
    low_list = []
    for source in range(layers):
        back = None
        for target in range(source, layers):
            product = lax.dot_general(
                errors[target],
                dec_weight[pair_index(source, target, layers)],
                (((1,), (1,)), ((), ())),
                preferred_element_type=f32,
            )
            back = product if back is None else back + product
        unused, pullback = jax.vjp(activate, pre_list[source])
        dpre = pullback(back)[0]
        grad_ebias_list.append(jnp.sum(dpre, axis=0))
        low_list.append(dpre.astype(bf16))
    slot_dpre = lax.dot_general(
        pick.astype(bf16),
        jnp.concatenate(low_list, axis=1),
        (((0,), (0,)), ((), ())),
        preferred_element_type=f32,
    ).astype(bf16)
    grad_enc = jnp.stack(
        [
            lax.dot_general(
                slots[source],
                slot_dpre[:, source * wide : (source + 1) * wide],
                (((0,), (0,)), ((), ())),
                preferred_element_type=f32,
            ).astype(bf16)
            for source in range(layers)
        ],
        axis=0,
    )
    grad_ebias = jnp.stack(grad_ebias_list, axis=0)
    return (jnp.transpose(rebuilt, (1, 0, 2)), grad_enc, grad_ebias, grad_dec, grad_dbias)


def solution(mesh):
    in_specs = (
        P(("groups", "latent"), None, None),
        P("groups"),
        P(("groups", "latent"), None, None),
        P("groups", None, "latent"),
        P("groups", "latent"),
        P("groups", "latent", None),
        P("groups", None),
    )
    out_specs = (
        P(("groups", "latent"), None, None),
        P("groups", None, "latent"),
        P("groups", "latent"),
        P("groups", "latent", None),
        P("groups", None),
    )
    return jax.shard_map(
        functools.partial(body, mesh.shape["latent"]),
        mesh=mesh,
        in_specs=in_specs,
        out_specs=out_specs,
        check_vma=False,
    )
```
